512 devices in a mesh: row: 32 (over x, y, core), col: 16 (over z).
Axes of the slice: x: 4, y: 4, z: 16, core: 2. Of those that a mesh axis runs over, the one named last changes fastest.
Arguments:
- inputs: bfloat16 [2048, 8192], P('row', 'col'), may hold values from -6 to 6
- gate_pre: bfloat16 [2048, 16384], P('col', 'row'), may hold values from -8 to 8
- up_pre: bfloat16 [2048, 16384], P('col', 'row'), may hold values from -6 to 6
- w_gate: bfloat16 [8192, 16384], P('col', 'row'), may hold values from -0.0625 to 0.0625
- w_up: bfloat16 [8192, 16384], P('col', 'row'), may hold values from -0.0625 to 0.0625
- w_down: bfloat16 [16384, 8192], P('row', 'col'), may hold values from -0.046875 to 0.046875
- grad_out: bfloat16 [2048, 8192], P('row', 'col'), may hold values from -2 to 2
Outputs:
- input_grad: bfloat16 [2048, 8192], P('row', 'col')
- w_gate_grad: bfloat16 [8192, 16384], P('col', 'row')
- w_up_grad: bfloat16 [8192, 16384], P('col', 'row')
- w_down_grad: bfloat16 [16384, 8192], P('row', 'col')
The draws below stay inside these ranges and needn't reach their ends.
All inputs are finite; a program needn't handle non-finite values.
Results may differ from the reference program's by a relative error of at most 0.03.
Values may be sent and summed in bfloat16 or wider, within the bound.
No kernel may reach another device: no remote copies, remote signals or barrier semaphores. Data moves between devices by JAX's collectives and lax.ppermute only.
A program may use at most 64 MiB of HBM per device.

```python
import jax
import jax.numpy as jnp
from jax import lax

D = 8192
FF = 16384
TOKENS = 2048
N_ROW = 32
N_COL = 16


def spiked(drawn, rng, source, target, blocks, factor):
    owner, partner = [(jnp.arange(drawn.shape[axis_at]) // (drawn.shape[axis_at] // blocks)).reshape([-1 if axis == axis_at else 1 for axis in range(drawn.ndim)]) for axis_at in (source, target)]
    chosen = jax.random.permutation(rng, blocks)[partner]
    strong = (owner == chosen) | (owner == (partner + blocks // 2) % blocks)
    return jnp.where(strong, factor * drawn, drawn)


def levels(key, extent, cuts, low, largest):
    level, own = 1.0, jax.random.fold_in(key, 6)
    for dim, blocks in cuts:
        steps = jnp.exp(jax.random.uniform(jax.random.fold_in(own, dim), (blocks,), jnp.float32, low / len(cuts), largest / len(cuts)))
        level = level * jnp.repeat(steps, extent[dim] // blocks).reshape([-1 if axis == dim else 1 for axis in range(len(extent))])
    return level


def scatter_about(rng, dims, scale, bound, shards=(), kind=jnp.bfloat16):
    loudness = levels(rng, dims, shards, -0.22, 0.18) if shards else 1.0
    values = jax.random.normal(rng, dims, jnp.float32) * scale * loudness
    return jnp.minimum(jnp.maximum(values, -bound), bound).astype(kind)


def gaussian_with(stream_key, dims, deviation, reach, cuts, heavy, dtype=jnp.bfloat16):
    values = deviation * jax.random.normal(stream_key, dims, jnp.float32)
    if cuts:
        values = values * levels(stream_key, dims, cuts, -0.22, 0.18)
    return jnp.clip(spiked(values, jax.random.fold_in(stream_key, 3), *heavy), -reach, reach).astype(dtype)


def setup_inputs(seed: int = 0) -> dict:
    seeds = jax.random.split(jax.random.key(seed), 8)
    return {
        "inputs": scatter_about(seeds[0], (TOKENS, D), 1.0, 6.0, ((0, 32), (1, 16))),
        "gate_pre": scatter_about(seeds[1], (TOKENS, FF), 1.5, 8.0, ((0, 16), (1, 32))),
        "up_pre": scatter_about(seeds[2], (TOKENS, FF), 1.0, 6.0, ((0, 16), (1, 32))),
        "w_gate": scatter_about(seeds[3], (D, FF), D ** -0.5, 0.0625, ((0, 16), (1, 32))),
        "w_up": scatter_about(seeds[4], (D, FF), D ** -0.5, 0.0625, ((0, 16), (1, 32))),
        "w_down": scatter_about(seeds[5], (FF, D), FF ** -0.5, 0.046875, ((0, 32), (1, 16))),
        "grad_out": gaussian_with(seeds[6], (TOKENS, D), 0.25, 2.0, ((0, 32), (1, 16)), (1, 0, 32, 2.75)),
    }


def blocked_sum(left, right, blocks):
    rows = left.shape[1]
    cols = right.shape[1]
    ndims = (((1,), (1,)), ((), ()))

    def add_block(total, pair):
        part = lax.dot_general(pair[0], pair[1], ndims, preferred_element_type=jnp.float32)
        part = lax.optimization_barrier(part.astype(jnp.bfloat16))
        return total + part.astype(jnp.float32), None

    start = jnp.zeros((rows, cols), jnp.float32)
    total, _ = lax.scan(add_block, start, (left, right))
    return total


def split_last(array, blocks):
    lead, width = array.shape
    return array.reshape(lead, blocks, width // blocks).transpose(1, 0, 2)


def reference(inputs, gate_pre, up_pre, w_gate, w_up, w_down, grad_out):
    down_grad = blocked_sum(split_last(grad_out, N_COL), split_last(w_down, N_COL), N_COL)
    gate_val = gate_pre.astype(jnp.float32)
    up_val = up_pre.astype(jnp.float32)
    sigma = jax.nn.sigmoid(gate_val)
    active = gate_val * sigma
    hidden = (active * up_val).astype(jnp.bfloat16)
    gate_grad = (down_grad * up_val * sigma * (1.0 + gate_val * (1.0 - sigma))).astype(jnp.bfloat16)
    up_grad = (down_grad * active).astype(jnp.bfloat16)
    tdims = (((0,), (0,)), ((), ()))
    w_down_grad = lax.dot_general(hidden, grad_out, tdims, preferred_element_type=jnp.float32).astype(jnp.bfloat16)
    w_gate_grad = lax.dot_general(inputs, gate_grad, tdims, preferred_element_type=jnp.float32).astype(jnp.bfloat16)
    w_up_grad = lax.dot_general(inputs, up_grad, tdims, preferred_element_type=jnp.float32).astype(jnp.bfloat16)
    both_grads = jnp.concatenate((split_last(gate_grad, N_ROW), split_last(up_grad, N_ROW)), axis=2)
    both_weights = jnp.concatenate((split_last(w_gate, N_ROW), split_last(w_up, N_ROW)), axis=2)
    input_grad = blocked_sum(both_grads, both_weights, N_ROW)
    return input_grad.astype(jnp.bfloat16), w_gate_grad, w_up_grad, w_down_grad
```

```python
import jax
import jax.numpy as jnp
from jax import lax
from jax.sharding import PartitionSpec as P

F32 = jnp.float32
BF16 = jnp.bfloat16
NDIMS = (((1,), (1,)), ((), ()))
TDIMS = (((0,), (0,)), ((), ()))


def local(n_row, n_col, inputs, gate_pre, up_pre, w_gate, w_up, w_down, grad_out):
    chips = n_row // 2
    half = n_col // 2
    core = lax.axis_index("row") % 2
    col = lax.axis_index("col")
    siblings = [(i, i ^ 1) for i in range(n_row)]
    groups = [[2 * i + c for i in range(chips)] for c in range(2)]
    tokens = inputs.shape[0]
    units = w_gate.shape[1]

    def swap(array):
        return lax.ppermute(array, "row", siblings)

    def hop(array, step):
        return lax.ppermute(array, "col", [(i, (i + step) % n_col) for i in range(n_col)])

    def exchange(array):
        return lax.all_to_all(array, "row", 0, 0, axis_index_groups=groups, tiled=True)

    def chunk(array, index):
        return lax.dynamic_slice_in_dim(array, (index % n_col) * tokens, tokens, 0)

    acts = jnp.concatenate((gate_pre, up_pre), axis=1)
    keep = lax.dynamic_slice_in_dim(acts, core * tokens, tokens, 0)
    give = lax.dynamic_slice_in_dim(acts, (1 - core) * tokens, tokens, 0)
    acts = jnp.concatenate((keep, swap(give)), axis=1)
    acts_all = lax.all_gather(acts, "col", axis=0, tiled=True)
    w_down2 = jnp.concatenate((w_down, swap(w_down)), axis=0)

    cot = exchange(jnp.tile(grad_out, (chips, 1)))
    partial = lax.dot_general(cot, w_down2, NDIMS, preferred_element_type=F32).astype(BF16)

    up_sum = chunk(partial, col + half)
    down_sum = chunk(partial, col - half + 1)
    for step in range(1, half + 1):
        up_in = hop(up_sum, 1)
        if step < half:
            down_in = hop(down_sum, -1)
            up_sum = (up_in.astype(F32) + chunk(partial, col + half - step).astype(F32)).astype(BF16)
            if step < half - 1:
                own = chunk(partial, col - half + 1 + step).astype(F32)
                down_sum = (down_in.astype(F32) + own).astype(BF16)
            else:
                down_sum = down_in
    mine = up_in.astype(F32) + down_sum.astype(F32) + chunk(partial, col).astype(F32)
    mine = mine.astype(BF16)

    down_grad = jnp.zeros((n_col * tokens, 2 * units), BF16)

    def put(whole, piece, index):
        return lax.dynamic_update_slice_in_dim(whole, piece, (index % n_col) * tokens, 0)

    down_grad = put(down_grad, mine, col)
    above = below = mine
    for step in range(1, half + 1):
        above = hop(above, 1)
        if step < half:
            below = hop(below, -1)
        down_grad = put(down_grad, above, col - step)
        if step < half:
            down_grad = put(down_grad, below, col + step)

    w_gate2 = jnp.concatenate((w_gate, swap(w_gate)), axis=1)
    w_up2 = jnp.concatenate((w_up, swap(w_up)), axis=1)
    input_rows = lax.all_gather(inputs, "row", axis=0, tiled=True, axis_index_groups=groups)

    parts = [acts_all[:, i * units : (i + 1) * units].astype(F32) for i in range(4)]
    gate_val = jnp.concatenate((parts[0], parts[2]), axis=1)
    up_val = jnp.concatenate((parts[1], parts[3]), axis=1)
    sigma = jax.nn.sigmoid(gate_val)
    active = gate_val * sigma
    hidden = (active * up_val).astype(BF16)
    grads = down_grad.astype(F32)
    gate_grad = (grads * up_val * sigma * (1.0 + gate_val * (1.0 - sigma))).astype(BF16)
    up_grad = (grads * active).astype(BF16)

    wd = lax.dot_general(hidden, cot, TDIMS, preferred_element_type=F32)
    w_down_grad = (wd[:units] + swap(wd[units:].astype(BF16)).astype(F32)).astype(BF16)
    total = lax.dot_general(gate_grad, w_gate2, NDIMS, preferred_element_type=F32)
    total = total + lax.dot_general(up_grad, w_up2, NDIMS, preferred_element_type=F32)
    sums = exchange(total.astype(BF16)).reshape(chips, tokens, -1)
    input_grad = jnp.sum(sums.astype(F32), axis=0).astype(BF16)
    wg = lax.dot_general(input_rows, gate_grad, TDIMS, preferred_element_type=F32)
    wu = lax.dot_general(input_rows, up_grad, TDIMS, preferred_element_type=F32)
    other = swap(jnp.concatenate((wg[:, units:], wu[:, units:]), axis=0).astype(BF16)).astype(F32)
    rows = wg.shape[0]
    w_gate_grad = (wg[:, :units] + other[:rows]).astype(BF16)
    w_up_grad = (wu[:, :units] + other[rows:]).astype(BF16)
    return (input_grad, w_gate_grad, w_up_grad, w_down_grad)


def solution(mesh):
    n_row, n_col = mesh.shape["row"], mesh.shape["col"]

    def step(*arrays):
        return local(n_row, n_col, *arrays)

    return jax.shard_map(
        step,
        mesh=mesh,
        in_specs=(
            P("row", "col"),
            P("col", "row"),
            P("col", "row"),
            P("col", "row"),
            P("col", "row"),
            P("row", "col"),
            P("row", "col"),
        ),
        out_specs=(P("row", "col"), P("col", "row"), P("col", "row"), P("row", "col")),
        check_vma=False,
    )
```

```python
import jax
import jax.numpy as jnp
from jax import lax
from jax.experimental import pallas as pl
from jax.experimental.pallas import tpu as pltpu
from jax.sharding import PartitionSpec as P

F32 = jnp.float32
BF16 = jnp.bfloat16
NDIMS = (((1,), (1,)), ((), ()))
TDIMS = (((0,), (0,)), ((), ()))


def factors_kernel(acts_ref, gate_ref, up_ref, hidden_ref):
    units = acts_ref.shape[1] // 4
    for i in range(2):
        gate_val = acts_ref[:, 2 * i * units : (2 * i + 1) * units].astype(F32)
        up_val = acts_ref[:, (2 * i + 1) * units : (2 * i + 2) * units].astype(F32)
        sigma = jax.nn.sigmoid(gate_val)
        active = gate_val * sigma
        at = slice(i * units, (i + 1) * units)
        hidden_ref[:, at] = (active * up_val).astype(BF16)
        up_ref[:, at] = active.astype(BF16)
        gate_ref[:, at] = (up_val * sigma * (1.0 + gate_val * (1.0 - sigma))).astype(BF16)


def factors(acts, units):
    rows, block = acts.shape[0], 128
    out = jax.ShapeDtypeStruct((rows, 2 * units), BF16)
    spec = pl.BlockSpec((block, 2 * units), lambda i: (i, 0))
    return pl.pallas_call(
        factors_kernel,
        grid=(rows // block,),
        in_specs=[pl.BlockSpec((block, 4 * units), lambda i: (i, 0))],
        out_specs=[spec] * 3,
        out_shape=[out] * 3,
        compiler_params=pltpu.CompilerParams(vmem_limit_bytes=16 * 1024 * 1024),
        cost_estimate=pl.CostEstimate(
            flops=12 * rows * 2 * units,
            bytes_accessed=10 * rows * 2 * units,
            transcendentals=rows * 2 * units,
        ),
    )(acts)


def local(n_row, n_col, inputs, gate_pre, up_pre, w_gate, w_up, w_down, grad_out):
    chips = n_row // 2
    chip = lax.axis_index("row") // 2
    core = lax.axis_index("row") % 2
    col = lax.axis_index("col")
    siblings = [(i, i ^ 1) for i in range(n_row)]
    groups = [[2 * i + c for i in range(chips)] for c in range(2)]
    tokens = inputs.shape[0]
    units = w_gate.shape[1]

    def swap(array):
        return lax.ppermute(array, "row", siblings)

    def hop(array, step):
        return lax.ppermute(array, "col", [(i, (i + step) % n_col) for i in range(n_col)])

    def exchange(array):
        return lax.all_to_all(array, "row", 0, 0, axis_index_groups=groups, tiled=True)

    aligned = (chip + col) % 2 == 0
    moves = [
        ((2 * r + c) * n_col + z, (2 * (r ^ 1) + c) * n_col + (z - 1) % n_col)
        for r in range(chips)
        for c in range(2)
        for z in range(n_col)
        if (r + z) % 2
    ]
    moved = lax.ppermute(grad_out, ("row", "col"), moves)
    moved = jnp.where(aligned, grad_out, moved)
    spread = jnp.broadcast_to(moved[None], (chips,) + moved.shape).reshape(-1, moved.shape[1])
    acts = jnp.concatenate((gate_pre, up_pre), axis=1)
    spread, acts = lax.optimization_barrier((spread, acts))
    cot = exchange(spread)
    w_next = hop(w_down, -1)
    w_here = jnp.concatenate((w_down, swap(w_down)), axis=0)

    keep = lax.dynamic_slice_in_dim(acts, core * tokens, tokens, 0)
    give = lax.dynamic_slice_in_dim(acts, (1 - core) * tokens, tokens, 0)
    acts = jnp.concatenate((keep, swap(give)), axis=1)
    cot, w_next, acts, w_here = lax.optimization_barrier((cot, w_next, acts, w_here))
    acts_all = lax.all_gather(acts, "col", axis=0, tiled=True)
    w_next = jnp.concatenate((w_next, swap(w_next)), axis=0)
    cot = cot.reshape(n_col // 2, 2, tokens, -1)

    def pick(which):
        return lax.dynamic_index_in_dim(cot, which, 1, False).reshape(n_col // 2 * tokens, -1)

    partial = lax.dot_general(pick(col % 2), w_here, NDIMS, preferred_element_type=F32)
    partial = partial + lax.dot_general(
        pick(1 - col % 2), w_next, NDIMS, preferred_element_type=F32
    )
    partial = partial.astype(BF16)

    w_both = jnp.concatenate((w_gate, w_up), axis=0)
    partial, w_both = lax.optimization_barrier((partial, w_both))
    w_both = jnp.concatenate((w_both, swap(w_both)), axis=1)

    planes = n_col // 2
    half = planes // 2
    rank = col // 2

    def chunk(index):
        start = (index + planes) % planes * tokens
        return lax.dynamic_slice_in_dim(partial, start, tokens, 0).astype(F32)

    up_sum = chunk(rank + half).astype(BF16)
    down_grad = jnp.zeros((n_col * tokens, 2 * units), BF16)
    down_sum = chunk(rank - half + 1).astype(BF16)
    for step in range(1, half + 1):
        up_in = hop(up_sum, 2)
        if step == 2:
            down_sum, w_both, down_grad = lax.optimization_barrier((down_sum, w_both, down_grad))
        if step < half:
            down_in = hop(down_sum, -2)
            up_sum = (up_in.astype(F32) + chunk(rank + half - step)).astype(BF16)
            if step < half - 1:
                down_sum = (down_in.astype(F32) + chunk(rank - half + 1 + step)).astype(BF16)
    w_gate2, w_up2 = w_both[: w_gate.shape[0]], w_both[w_gate.shape[0] :]
    mine = (up_in.astype(F32) + down_in.astype(F32) + chunk(rank)).astype(BF16)

    rows = jnp.concatenate((inputs, grad_out), axis=1)
    rows = lax.all_gather(rows, "row", axis=0, tiled=True, axis_index_groups=groups)
    input_rows, cot_rows = rows[:, : inputs.shape[1]], rows[:, inputs.shape[1] :]

    gate_by, up_by, hidden = factors(acts_all, units)

    half = n_col // 2

    def put(whole, piece, index):
        start = (index + n_col) % n_col * tokens
        return lax.dynamic_update_slice_in_dim(whole, piece, start, 0)

    down_grad = put(down_grad, mine, col)
    above = below = mine
    for step in range(1, half + 1):
        above = hop(above, 1)
        if step == half - 1:
            below, gate_by, up_by, hidden = lax.optimization_barrier(
                (below, gate_by, up_by, hidden)
            )
        if step < half:
            below = hop(below, -1)
        down_grad = put(down_grad, above, col - step)
        if step < half:
            down_grad = put(down_grad, below, col + step)

    grads = down_grad.astype(F32)
    gate_grad = (grads * gate_by.astype(F32)).astype(BF16)
    up_grad = (grads * up_by.astype(F32)).astype(BF16)
    total = lax.dot_general(gate_grad, w_gate2, NDIMS, preferred_element_type=F32)
    total = total + lax.dot_general(up_grad, w_up2, NDIMS, preferred_element_type=F32)
    total, gate_grad, up_grad = lax.optimization_barrier(
        (total.astype(BF16), gate_grad, up_grad)
    )
    sums = exchange(total).reshape(chips, tokens, -1)
    input_grad = jnp.sum(sums.astype(F32), axis=0).astype(BF16)
    wd = lax.dot_general(hidden, cot_rows, TDIMS, preferred_element_type=F32)
    w_down_grad = (wd[:units] + swap(wd[units:].astype(BF16)).astype(F32)).astype(BF16)
    wg = lax.dot_general(input_rows, gate_grad, TDIMS, preferred_element_type=F32)
    wu = lax.dot_general(input_rows, up_grad, TDIMS, preferred_element_type=F32)
    other = swap(jnp.concatenate((wg[:, units:], wu[:, units:]), axis=0).astype(BF16)).astype(F32)
    width = wg.shape[0]
    w_gate_grad = (wg[:, :units] + other[:width]).astype(BF16)
    w_up_grad = (wu[:, :units] + other[width:]).astype(BF16)
    return (input_grad, w_gate_grad, w_up_grad, w_down_grad)


def solution(mesh):
    n_row, n_col = mesh.shape["row"], mesh.shape["col"]

    def step(*arrays):
        return local(n_row, n_col, *arrays)

    return jax.shard_map(
        step,
        mesh=mesh,
        in_specs=(
            P("row", "col"),
            P("col", "row"),
            P("col", "row"),
            P("col", "row"),
            P("col", "row"),
            P("row", "col"),
            P("row", "col"),
        ),
        out_specs=(P("row", "col"), P("col", "row"), P("col", "row"), P("row", "col")),
        check_vma=False,
    )
```

```python
import jax
import jax.numpy as jnp
from jax import lax
from jax.experimental import pallas as pl
from jax.experimental.pallas import tpu as pltpu
from jax.sharding import PartitionSpec as P

F32 = jnp.float32
BF16 = jnp.bfloat16
NDIMS = (((1,), (1,)), ((), ()))
TDIMS = (((0,), (0,)), ((), ()))


def factors_kernel(acts_ref, gate_ref, up_ref, hidden_ref):
    units = acts_ref.shape[1] // 4
    for i in range(2):
        gate_val = acts_ref[:, 2 * i * units : (2 * i + 1) * units].astype(F32)
        up_val = acts_ref[:, (2 * i + 1) * units : (2 * i + 2) * units].astype(F32)
        sigma = jax.nn.sigmoid(gate_val)
        active = gate_val * sigma
        at = slice(i * units, (i + 1) * units)
        hidden_ref[:, at] = (active * up_val).astype(BF16)
        up_ref[:, at] = active.astype(BF16)
        gate_ref[:, at] = (up_val * sigma * (1.0 + gate_val * (1.0 - sigma))).astype(BF16)


def factors(acts, units):
    rows, block = acts.shape[0], 128
    out = jax.ShapeDtypeStruct((rows, 2 * units), BF16)
    spec = pl.BlockSpec((block, 2 * units), lambda i: (i, 0))
    return pl.pallas_call(
        factors_kernel,
        grid=(rows // block,),
        in_specs=[pl.BlockSpec((block, 4 * units), lambda i: (i, 0))],
        out_specs=[spec] * 3,
        out_shape=[out] * 3,
        compiler_params=pltpu.CompilerParams(vmem_limit_bytes=16 * 1024 * 1024),
        cost_estimate=pl.CostEstimate(
            flops=12 * rows * 2 * units,
            bytes_accessed=10 * rows * 2 * units,
            transcendentals=rows * 2 * units,
        ),
    )(acts)


def local(n_row, n_col, inputs, gate_pre, up_pre, w_gate, w_up, w_down, grad_out):
    chips = n_row // 2
    chip = lax.axis_index("row") // 2
    core = lax.axis_index("row") % 2
    col = lax.axis_index("col")
    siblings = [(i, i ^ 1) for i in range(n_row)]
    groups = [[2 * i + c for i in range(chips)] for c in range(2)]
    tokens = inputs.shape[0]
    units = w_gate.shape[1]

    def swap(array):
        return lax.ppermute(array, "row", siblings)

    def hop(array, step):
        return lax.ppermute(array, "col", [(i, (i + step) % n_col) for i in range(n_col)])

    def exchange(array):
        return lax.all_to_all(array, "row", 0, 0, axis_index_groups=groups, tiled=True)

    aligned = (chip + col) % 2 == 0
    moves = [
        ((2 * r + c) * n_col + z, (2 * (r ^ 1) + c) * n_col + (z + 1) % n_col)
        for r in range(chips)
        for c in range(2)
        for z in range(n_col)
        if (r + z) % 2
    ]
    moved = lax.ppermute(grad_out, ("row", "col"), moves)
    moved = jnp.where(aligned, grad_out, moved)
    spread = jnp.broadcast_to(moved[None], (chips,) + moved.shape).reshape(-1, moved.shape[1])
    acts = jnp.concatenate((gate_pre, up_pre), axis=1)
    spread, acts = lax.optimization_barrier((spread, acts))
    cot = exchange(spread)
    w_next = hop(w_down, 1)
    w_here = jnp.concatenate((w_down, swap(w_down)), axis=0)

    keep = lax.dynamic_slice_in_dim(acts, core * tokens, tokens, 0)
    give = lax.dynamic_slice_in_dim(acts, (1 - core) * tokens, tokens, 0)
    acts = jnp.concatenate((keep, swap(give)), axis=1)
    cot, w_next, acts, w_here = lax.optimization_barrier((cot, w_next, acts, w_here))
    acts_all = lax.all_gather(acts, "col", axis=0, tiled=True)
    w_next = jnp.concatenate((w_next, swap(w_next)), axis=0)
    cot = cot.reshape(n_col // 2, 2, tokens, -1)

    def pick(which):
        return lax.dynamic_index_in_dim(cot, which, 1, False).reshape(n_col // 2 * tokens, -1)

    partial = lax.dot_general(pick(col % 2), w_here, NDIMS, preferred_element_type=F32)
    partial = partial + lax.dot_general(
        pick(1 - col % 2), w_next, NDIMS, preferred_element_type=F32
    )
    partial = partial.astype(BF16)

    w_both = jnp.concatenate((w_gate, w_up), axis=0)
    partial, w_both = lax.optimization_barrier((partial, w_both))
    w_both = jnp.concatenate((w_both, swap(w_both)), axis=1)

    planes = n_col // 2
    half = planes // 2
    rank = col // 2

    def chunk(index):
        start = (index + planes) % planes * tokens
        return lax.dynamic_slice_in_dim(partial, start, tokens, 0).astype(F32)

    up_sum = chunk(rank + half).astype(BF16)
    down_grad = jnp.zeros((n_col * tokens, 2 * units), BF16)
    down_sum = chunk(rank - half + 1).astype(BF16)
    for step in range(1, half + 1):
        up_in = hop(up_sum, 2)
        if step == 2:
            down_sum, w_both, down_grad = lax.optimization_barrier((down_sum, w_both, down_grad))
        if step < half:
            down_in = hop(down_sum, -2)
            up_sum = (up_in.astype(F32) + chunk(rank + half - step)).astype(BF16)
            if step < half - 1:
                down_sum = (down_in.astype(F32) + chunk(rank - half + 1 + step)).astype(BF16)
    w_gate2, w_up2 = w_both[: w_gate.shape[0]], w_both[w_gate.shape[0] :]
    mine = (up_in.astype(F32) + down_in.astype(F32) + chunk(rank)).astype(BF16)

    rows = jnp.concatenate((inputs, grad_out), axis=1)
    rows = lax.all_gather(rows, "row", axis=0, tiled=True, axis_index_groups=groups)
    input_rows, cot_rows = rows[:, : inputs.shape[1]], rows[:, inputs.shape[1] :]

    gate_by, up_by, hidden = factors(acts_all, units)

    half = n_col // 2

    def put(whole, piece, index):
        start = (index + n_col) % n_col * tokens
        return lax.dynamic_update_slice_in_dim(whole, piece, start, 0)

    down_grad = put(down_grad, mine, col)
    above = below = mine
    for step in range(1, half + 1):
        above = hop(above, 1)
        if step == half:
            above, gate_by, up_by, hidden = lax.optimization_barrier(
                (above, gate_by, up_by, hidden)
            )
        if step < half:
            below = hop(below, -1)
        down_grad = put(down_grad, above, col - step)
        if step < half:
            down_grad = put(down_grad, below, col + step)

    grads = down_grad.astype(F32)
    gate_grad = (grads * gate_by.astype(F32)).astype(BF16)
    up_grad = (grads * up_by.astype(F32)).astype(BF16)
    total = lax.dot_general(gate_grad, w_gate2, NDIMS, preferred_element_type=F32)
    total = total + lax.dot_general(up_grad, w_up2, NDIMS, preferred_element_type=F32)
    total, gate_grad, up_grad = lax.optimization_barrier(
        (total.astype(BF16), gate_grad, up_grad)
    )
    sums = exchange(total).reshape(chips, tokens, -1)
    input_grad = jnp.sum(sums.astype(F32), axis=0).astype(BF16)
    total, gate_grad, up_grad = lax.optimization_barrier(
        (total.astype(BF16), gate_grad, up_grad)
    )
    sums = exchange(total).reshape(chips, tokens, -1)
    input_grad = jnp.sum(sums.astype(F32), axis=0).astype(BF16)
    wd = lax.dot_general(hidden, cot_rows, TDIMS, preferred_element_type=F32)
    w_down_grad = (wd[:units] + swap(wd[units:].astype(BF16)).astype(F32)).astype(BF16)

    def over_tokens(left, right):
        return lax.dot_general(left, right, TDIMS, preferred_element_type=F32)

    wd_other = swap(over_tokens(hidden[:, units:], cot_rows).astype(BF16))
    wg_give = over_tokens(input_rows, gate_grad[:, units:]).astype(BF16)
    wu_give = over_tokens(input_rows, up_grad[:, units:]).astype(BF16)
    width = wg_give.shape[0]
    other = swap(jnp.concatenate((wg_give, wu_give), axis=0))
    w_down_grad = (over_tokens(hidden[:, :units], cot_rows) + wd_other.astype(F32)).astype(BF16)
    w_gate_grad = over_tokens(input_rows, gate_grad[:, :units]) + other[:width].astype(F32)
    w_up_grad = over_tokens(input_rows, up_grad[:, :units]) + other[width:].astype(F32)
    w_gate_grad, w_up_grad = w_gate_grad.astype(BF16), w_up_grad.astype(BF16)
    return (input_grad, w_gate_grad, w_up_grad, w_down_grad)


def solution(mesh):
    n_row, n_col = mesh.shape["row"], mesh.shape["col"]

    def step(*arrays):
        return local(n_row, n_col, *arrays)

    return jax.shard_map(
        step,
        mesh=mesh,
        in_specs=(
            P("row", "col"),
            P("col", "row"),
            P("col", "row"),
            P("col", "row"),
            P("col", "row"),
            P("row", "col"),
            P("row", "col"),
        ),
        out_specs=(P("row", "col"), P("col", "row"), P("col", "row"), P("row", "col")),
        check_vma=False,
    )
```

```python
import jax
import jax.numpy as jnp
from jax import lax
from jax.experimental import pallas as pl
from jax.experimental.pallas import tpu as pltpu
from jax.sharding import PartitionSpec as P

F32 = jnp.float32
BF16 = jnp.bfloat16
NDIMS = (((1,), (1,)), ((), ()))


def factors_kernel(acts_ref, gate_ref, up_ref, hidden_ref):
    units = acts_ref.shape[1] // 4
    for i in range(2):
        gate_val = acts_ref[:, 2 * i * units : (2 * i + 1) * units].astype(F32)
        up_val = acts_ref[:, (2 * i + 1) * units : (2 * i + 2) * units].astype(F32)
        sigma = jax.nn.sigmoid(gate_val)
        active = gate_val * sigma
        at = slice(i * units, (i + 1) * units)
        hidden_ref[at, :] = (active * up_val).T.astype(BF16)
        up_ref[:, at] = active.astype(BF16)
        gate_ref[:, at] = (up_val * sigma * (1.0 + gate_val * (1.0 - sigma))).astype(BF16)


def factors(acts, units):
    rows, block = acts.shape[0], 128
    out = jax.ShapeDtypeStruct((rows, 2 * units), BF16)
    spec = pl.BlockSpec((block, 2 * units), lambda i: (i, 0))
    return pl.pallas_call(
        factors_kernel,
        grid=(rows // block,),
        in_specs=[pl.BlockSpec((block, 4 * units), lambda i: (i, 0))],
        out_specs=[spec, spec, pl.BlockSpec((2 * units, block), lambda i: (0, i))],
        out_shape=[out, out, jax.ShapeDtypeStruct((2 * units, rows), BF16)],
        compiler_params=pltpu.CompilerParams(vmem_limit_bytes=16 * 1024 * 1024),
        cost_estimate=pl.CostEstimate(
            flops=12 * rows * 2 * units,
            bytes_accessed=10 * rows * 2 * units,
            transcendentals=rows * 2 * units,
        ),
    )(acts)


def local(n_row, n_col, inputs, gate_pre, up_pre, w_gate, w_up, w_down, grad_out):
    chips = n_row // 2
    chip = lax.axis_index("row") // 2
    core = lax.axis_index("row") % 2
    col = lax.axis_index("col")
    siblings = [(i, i ^ 1) for i in range(n_row)]
    groups = [[2 * i + c for i in range(chips)] for c in range(2)]
    tokens = inputs.shape[0]
    units = w_gate.shape[1]

    def swap(array):
        return lax.ppermute(array, "row", siblings)

    def hop(array, step):
        return lax.ppermute(array, "col", [(i, (i + step) % n_col) for i in range(n_col)])

    def exchange(array):
        return lax.all_to_all(array, "row", 0, 0, axis_index_groups=groups, tiled=True)

    aligned = (chip + col) % 2 == 0
    moves = [
        ((2 * r + c) * n_col + z, (2 * (r ^ 1) + c) * n_col + (z + 1) % n_col)
        for r in range(chips)
        for c in range(2)
        for z in range(n_col)
        if (r + z) % 2
    ]
    moved = lax.ppermute(grad_out, ("row", "col"), moves)
    moved = jnp.where(aligned, grad_out, moved)
    spread = jnp.broadcast_to(moved[None], (chips,) + moved.shape).reshape(-1, moved.shape[1])
    acts = jnp.concatenate((gate_pre, up_pre), axis=1)
    spread, acts = lax.optimization_barrier((spread, acts))
    cot = exchange(spread)
    w_next = hop(w_down, 1)
    w_here = jnp.concatenate((w_down, swap(w_down)), axis=0)

    keep = lax.dynamic_slice_in_dim(acts, core * tokens, tokens, 0)
    give = lax.dynamic_slice_in_dim(acts, (1 - core) * tokens, tokens, 0)
    acts = jnp.concatenate((keep, swap(give)), axis=1)
    cot, w_next, acts, w_here = lax.optimization_barrier((cot, w_next, acts, w_here))
    acts_all = lax.all_gather(acts, "col", axis=0, tiled=True)
    w_next = jnp.concatenate((w_next, swap(w_next)), axis=0)
    cot = cot.reshape(n_col // 2, 2, tokens, -1)

    def pick(which):
        return lax.dynamic_index_in_dim(cot, which, 1, False).reshape(n_col // 2 * tokens, -1)

    partial = lax.dot_general(pick(col % 2), w_here, NDIMS, preferred_element_type=F32)
    partial = partial + lax.dot_general(
        pick(1 - col % 2), w_next, NDIMS, preferred_element_type=F32
    )
    partial = partial.astype(BF16)

    w_both = jnp.concatenate((w_gate, w_up), axis=0)
    partial, w_both = lax.optimization_barrier((partial, w_both))
    w_both = jnp.concatenate((w_both, swap(w_both)), axis=1)

    planes = n_col // 2
    half = planes // 2
    rank = col // 2

    def chunk(index):
        start = (index + planes) % planes * tokens
        return lax.dynamic_slice_in_dim(partial, start, tokens, 0).astype(F32)

    up_sum = chunk(rank + half).astype(BF16)
    down_grad = jnp.zeros((n_col * tokens, 2 * units), BF16)
    down_sum = chunk(rank - half + 1).astype(BF16)
    for step in range(1, half + 1):
        up_in = hop(up_sum, 2)
        if step == 2:
            down_sum, w_both, down_grad = lax.optimization_barrier((down_sum, w_both, down_grad))
        if step < half:
            down_in = hop(down_sum, -2)
            up_sum = (up_in.astype(F32) + chunk(rank + half - step)).astype(BF16)
            if step < half - 1:
                down_sum = (down_in.astype(F32) + chunk(rank - half + 1 + step)).astype(BF16)
    w_gate2, w_up2 = w_both[: w_gate.shape[0]], w_both[w_gate.shape[0] :]
    mine = (up_in.astype(F32) + down_in.astype(F32) + chunk(rank)).astype(BF16)

    rows = jnp.concatenate((inputs, grad_out), axis=1)
    rows = lax.all_gather(rows, "row", axis=0, tiled=True, axis_index_groups=groups)
    input_rows, cot_rows = rows[:, : inputs.shape[1]], rows[:, inputs.shape[1] :]

    gate_by, up_by, hidden = factors(acts_all, units)

    half = n_col // 2

    def put(whole, piece, index):
        start = (index + n_col) % n_col * tokens
        return lax.dynamic_update_slice_in_dim(whole, piece, start, 0)

    down_grad = put(down_grad, mine, col)
    above = below = mine
    for step in range(1, half + 1):
        above = hop(above, 1)
        if step == half:
            above, gate_by, up_by, hidden = lax.optimization_barrier(
                (above, gate_by, up_by, hidden)
            )
        if step < half:
            below = hop(below, -1)
        down_grad = put(down_grad, above, col - step)
        if step < half:
            down_grad = put(down_grad, below, col + step)

    grads = down_grad.astype(F32)
    gate_grad = (grads * gate_by.astype(F32)).astype(BF16)
    up_grad = (grads * up_by.astype(F32)).astype(BF16)
    total = lax.dot_general(gate_grad, w_gate2, NDIMS, preferred_element_type=F32)
    total = total + lax.dot_general(up_grad, w_up2, NDIMS, preferred_element_type=F32)
    total, gate_grad, up_grad = lax.optimization_barrier(
        (total.astype(BF16), gate_grad, up_grad)
    )
    sums = exchange(total).reshape(chips, tokens, -1)
    input_grad = jnp.sum(sums.astype(F32), axis=0).astype(BF16)

    def over_tokens(left, right):
        return jnp.dot(left, right, preferred_element_type=F32)

    input_rows = lax.optimization_barrier(input_rows.T)
    wd_other = swap(over_tokens(hidden[units:], cot_rows).astype(BF16))
    wg_give = over_tokens(input_rows, gate_grad[:, units:]).astype(BF16)
    wu_give = over_tokens(input_rows, up_grad[:, units:]).astype(BF16)
    width = wg_give.shape[0]
    other = swap(jnp.concatenate((wg_give, wu_give), axis=0))
    w_down_grad = (over_tokens(hidden[:units], cot_rows) + wd_other.astype(F32)).astype(BF16)
    w_gate_grad = over_tokens(input_rows, gate_grad[:, :units]) + other[:width].astype(F32)
    w_up_grad = over_tokens(input_rows, up_grad[:, :units]) + other[width:].astype(F32)
    w_gate_grad, w_up_grad = w_gate_grad.astype(BF16), w_up_grad.astype(BF16)
    return (input_grad, w_gate_grad, w_up_grad, w_down_grad)


def solution(mesh):
    n_row, n_col = mesh.shape["row"], mesh.shape["col"]

    def step(*arrays):
        return local(n_row, n_col, *arrays)

    return jax.shard_map(
        step,
        mesh=mesh,
        in_specs=(
            P("row", "col"),
            P("col", "row"),
            P("col", "row"),
            P("col", "row"),
            P("col", "row"),
            P("row", "col"),
            P("row", "col"),
        ),
        out_specs=(P("row", "col"), P("col", "row"), P("col", "row"), P("row", "col")),
        check_vma=False,
    )
```

```python
import jax
import jax.numpy as jnp
from jax import lax
from jax.experimental import pallas as pl
from jax.experimental.pallas import tpu as pltpu
from jax.sharding import PartitionSpec as P

F32 = jnp.float32
BF16 = jnp.bfloat16
NDIMS = (((1,), (1,)), ((), ()))
TDIMS = (((0,), (0,)), ((), ()))


def factors_kernel(acts_ref, gate_ref, up_ref, hidden_ref):
    units = acts_ref.shape[1] // 4
    for i in range(2):
        gate_val = acts_ref[:, 2 * i * units : (2 * i + 1) * units].astype(F32)
        up_val = acts_ref[:, (2 * i + 1) * units : (2 * i + 2) * units].astype(F32)
        sigma = jax.nn.sigmoid(gate_val)
        active = gate_val * sigma
        at = slice(i * units, (i + 1) * units)
        hidden_ref[:, at] = (active * up_val).astype(BF16)
        up_ref[:, at] = active.astype(BF16)
        gate_ref[:, at] = (up_val * sigma * (1.0 + gate_val * (1.0 - sigma))).astype(BF16)


def factors(acts, units):
    rows, block = acts.shape[0], 128
    out = jax.ShapeDtypeStruct((rows, 2 * units), BF16)
    spec = pl.BlockSpec((block, 2 * units), lambda i: (i, 0))
    return pl.pallas_call(
        factors_kernel,
        grid=(rows // block,),
        in_specs=[pl.BlockSpec((block, 4 * units), lambda i: (i, 0))],
        out_specs=[spec] * 3,
        out_shape=[out] * 3,
        compiler_params=pltpu.CompilerParams(vmem_limit_bytes=16 * 1024 * 1024),
        cost_estimate=pl.CostEstimate(
            flops=12 * rows * 2 * units,
            bytes_accessed=10 * rows * 2 * units,
            transcendentals=rows * 2 * units,
        ),
    )(acts)


def local(n_row, n_col, inputs, gate_pre, up_pre, w_gate, w_up, w_down, grad_out):
    chips = n_row // 2
    chip = lax.axis_index("row") // 2
    core = lax.axis_index("row") % 2
    col = lax.axis_index("col")
    siblings = [(i, i ^ 1) for i in range(n_row)]
    groups = [[2 * i + c for i in range(chips)] for c in range(2)]
    tokens = inputs.shape[0]
    units = w_gate.shape[1]

    def swap(array):
        return lax.ppermute(array, "row", siblings)

    def hop(array, step):
        return lax.ppermute(array, "col", [(i, (i + step) % n_col) for i in range(n_col)])

    def exchange(array):
        return lax.all_to_all(array, "row", 0, 0, axis_index_groups=groups, tiled=True)

    aligned = (chip + col) % 2 == 0
    moves = [
        ((2 * r + c) * n_col + z, (2 * (r ^ 1) + c) * n_col + (z + 1) % n_col)
        for r in range(chips)
        for c in range(2)
        for z in range(n_col)
        if (r + z) % 2
    ]
    moved = lax.ppermute(grad_out, ("row", "col"), moves)
    moved = jnp.where(aligned, grad_out, moved)
    spread = jnp.broadcast_to(moved[None], (chips,) + moved.shape).reshape(-1, moved.shape[1])
    acts = jnp.concatenate((gate_pre, up_pre), axis=1)
    spread, acts = lax.optimization_barrier((spread, acts))
    cot = exchange(spread)
    w_next = hop(w_down, 1)
    w_here = jnp.concatenate((w_down, swap(w_down)), axis=0)

    keep = lax.dynamic_slice_in_dim(acts, core * tokens, tokens, 0)
    give = lax.dynamic_slice_in_dim(acts, (1 - core) * tokens, tokens, 0)
    acts = jnp.concatenate((keep, swap(give)), axis=1)
    cot, w_next, acts, w_here = lax.optimization_barrier((cot, w_next, acts, w_here))
    acts_all = lax.all_gather(acts, "col", axis=0, tiled=True)
    w_next = jnp.concatenate((w_next, swap(w_next)), axis=0)
    cot = cot.reshape(n_col // 2, 2, tokens, -1)

    def pick(which):
        return lax.dynamic_index_in_dim(cot, which, 1, False).reshape(n_col // 2 * tokens, -1)

    partial = lax.dot_general(pick(col % 2), w_here, NDIMS, preferred_element_type=F32)
    partial = partial + lax.dot_general(
        pick(1 - col % 2), w_next, NDIMS, preferred_element_type=F32
    )
    partial = partial.astype(BF16)

    w_both = jnp.concatenate((w_gate, w_up), axis=0)
    partial, w_both = lax.optimization_barrier((partial, w_both))
    w_both = jnp.concatenate((w_both, swap(w_both)), axis=1)

    planes = n_col // 2
    half = planes // 2
    rank = col // 2

    def chunk(index):
        start = (index + planes) % planes * tokens
        return lax.dynamic_slice_in_dim(partial, start, tokens, 0).astype(F32)

    up_sum = chunk(rank + half).astype(BF16)
    down_grad = jnp.zeros((n_col * tokens, 2 * units), BF16)
    down_sum = chunk(rank - half + 1).astype(BF16)
    for step in range(1, half + 1):
        up_in = hop(up_sum, 2)
        if step == 2:
            down_sum, w_both, down_grad = lax.optimization_barrier((down_sum, w_both, down_grad))
        if step < half:
            down_in = hop(down_sum, -2)
            up_sum = (up_in.astype(F32) + chunk(rank + half - step)).astype(BF16)
            if step < half - 1:
                down_sum = (down_in.astype(F32) + chunk(rank - half + 1 + step)).astype(BF16)
    w_gate2, w_up2 = w_both[: w_gate.shape[0]], w_both[w_gate.shape[0] :]
    mine = (up_in.astype(F32) + down_in.astype(F32) + chunk(rank)).astype(BF16)

    rows = jnp.concatenate((inputs, grad_out), axis=1)
    rows, _ = lax.optimization_barrier((rows, partial))
    rows = exchange(jnp.broadcast_to(rows[None], (chips,) + rows.shape).reshape(-1, rows.shape[1]))

    gate_by, up_by, hidden = factors(acts_all, units)

    half = n_col // 2

    def put(whole, piece, index):
        start = (index + n_col) % n_col * tokens
        return lax.dynamic_update_slice_in_dim(whole, piece, start, 0)

    down_grad = put(down_grad, mine, col)
    above = below = mine
    for step in range(1, half + 1):
        above = hop(above, 1)
        if step == half:
            above, gate_by, up_by, hidden = lax.optimization_barrier(
                (above, gate_by, up_by, hidden)
            )
        if step == 4:
            below, rows = lax.optimization_barrier((below, rows))
        if step < half:
            below = hop(below, -1)
        down_grad = put(down_grad, above, col - step)
        if step < half:
            down_grad = put(down_grad, below, col + step)

    input_rows, cot_rows = rows[:, : inputs.shape[1]], rows[:, inputs.shape[1] :]
    grads = down_grad.astype(F32)
    gate_grad = (grads * gate_by.astype(F32)).astype(BF16)
    up_grad = (grads * up_by.astype(F32)).astype(BF16)
    total = lax.dot_general(gate_grad, w_gate2, NDIMS, preferred_element_type=F32)
    total = total + lax.dot_general(up_grad, w_up2, NDIMS, preferred_element_type=F32)
    total, gate_grad, up_grad = lax.optimization_barrier(
        (total.astype(BF16), gate_grad, up_grad)
    )
    sums = exchange(total).reshape(chips, tokens, -1)
    input_grad = jnp.sum(sums.astype(F32), axis=0).astype(BF16)

    def over_tokens(left, right):
        return lax.dot_general(left, right, TDIMS, preferred_element_type=F32)

    wd_other = swap(over_tokens(hidden[:, units:], cot_rows).astype(BF16))
    wg_give = over_tokens(input_rows, gate_grad[:, units:]).astype(BF16)
    wu_give = over_tokens(input_rows, up_grad[:, units:]).astype(BF16)
    width = wg_give.shape[0]
    other = swap(jnp.concatenate((wg_give, wu_give), axis=0))
    w_down_grad = (over_tokens(hidden[:, :units], cot_rows) + wd_other.astype(F32)).astype(BF16)
    w_gate_grad = over_tokens(input_rows, gate_grad[:, :units]) + other[:width].astype(F32)
    w_up_grad = over_tokens(input_rows, up_grad[:, :units]) + other[width:].astype(F32)
    w_gate_grad, w_up_grad = w_gate_grad.astype(BF16), w_up_grad.astype(BF16)
    return (input_grad, w_gate_grad, w_up_grad, w_down_grad)


def solution(mesh):
    n_row, n_col = mesh.shape["row"], mesh.shape["col"]

    def step(*arrays):
        return local(n_row, n_col, *arrays)

    return jax.shard_map(
        step,
        mesh=mesh,
        in_specs=(
            P("row", "col"),
            P("col", "row"),
            P("col", "row"),
            P("col", "row"),
            P("col", "row"),
            P("row", "col"),
            P("row", "col"),
        ),
        out_specs=(P("row", "col"), P("col", "row"), P("col", "row"), P("row", "col")),
        check_vma=False,
    )
```

```python
import jax
import jax.numpy as jnp
from jax import lax
from jax.experimental import pallas as pl
from jax.experimental.pallas import tpu as pltpu
from jax.sharding import PartitionSpec as P

F32 = jnp.float32
BF16 = jnp.bfloat16
NDIMS = (((1,), (1,)), ((), ()))
TDIMS = (((0,), (0,)), ((), ()))


def factors_kernel(acts_ref, gate_ref, up_ref, hidden_ref):
    units = acts_ref.shape[1] // 4
    for i in range(2):
        gate_val = acts_ref[:, 2 * i * units : (2 * i + 1) * units].astype(F32)
        up_val = acts_ref[:, (2 * i + 1) * units : (2 * i + 2) * units].astype(F32)
        sigma = jax.nn.sigmoid(gate_val)
        active = gate_val * sigma
        at = slice(i * units, (i + 1) * units)
        hidden_ref[:, at] = (active * up_val).astype(BF16)
        up_ref[:, at] = active.astype(BF16)
        gate_ref[:, at] = (up_val * sigma * (1.0 + gate_val * (1.0 - sigma))).astype(BF16)


def factors(acts, units):
    rows, block = acts.shape[0], 128
    out = jax.ShapeDtypeStruct((rows, 2 * units), BF16)
    spec = pl.BlockSpec((block, 2 * units), lambda i: (i, 0))
    return pl.pallas_call(
        factors_kernel,
        grid=(rows // block,),
        in_specs=[pl.BlockSpec((block, 4 * units), lambda i: (i, 0))],
        out_specs=[spec] * 3,
        out_shape=[out] * 3,
        compiler_params=pltpu.CompilerParams(vmem_limit_bytes=16 * 1024 * 1024),
        cost_estimate=pl.CostEstimate(
            flops=12 * rows * 2 * units,
            bytes_accessed=10 * rows * 2 * units,
            transcendentals=rows * 2 * units,
        ),
    )(acts)


def local(n_row, n_col, inputs, gate_pre, up_pre, w_gate, w_up, w_down, grad_out):
    chips = n_row // 2
    chip = lax.axis_index("row") // 2
    core = lax.axis_index("row") % 2
    col = lax.axis_index("col")
    siblings = [(i, i ^ 1) for i in range(n_row)]
    groups = [[2 * i + c for i in range(chips)] for c in range(2)]
    tokens = inputs.shape[0]
    units = w_gate.shape[1]

    def swap(array):
        return lax.ppermute(array, "row", siblings)

    def hop(array, step):
        return lax.ppermute(array, "col", [(i, (i + step) % n_col) for i in range(n_col)])

    def exchange(array):
        return lax.all_to_all(array, "row", 0, 0, axis_index_groups=groups, tiled=True)

    aligned = (chip + col) % 2 == 0
    moves = [
        ((2 * r + c) * n_col + z, (2 * (r ^ 1) + c) * n_col + (z + 1) % n_col)
        for r in range(chips)
        for c in range(2)
        for z in range(n_col)
        if (r + z) % 2
    ]
    moved = lax.ppermute(grad_out, ("row", "col"), moves)
    moved = jnp.where(aligned, grad_out, moved)
    spread = jnp.broadcast_to(moved[None], (chips,) + moved.shape).reshape(-1, moved.shape[1])
    acts = jnp.concatenate((gate_pre, up_pre), axis=1)
    spread, acts = lax.optimization_barrier((spread, acts))
    cot = exchange(spread)
    w_next = hop(w_down, 1)
    w_here = jnp.concatenate((w_down, swap(w_down)), axis=0)

    keep = lax.dynamic_slice_in_dim(acts, core * tokens, tokens, 0)
    give = lax.dynamic_slice_in_dim(acts, (1 - core) * tokens, tokens, 0)
    acts = jnp.concatenate((keep, swap(give)), axis=1)
    cot, acts, w_here = lax.optimization_barrier((cot, acts, w_here))
    acts_all = lax.all_gather(acts, "col", axis=0, tiled=True)
    cot, w_next = lax.optimization_barrier((cot, w_next))
    w_next = jnp.concatenate((w_next, swap(w_next)), axis=0)
    cot = cot.reshape(n_col // 2, 2, tokens, -1)

    def pick(which):
        return lax.dynamic_index_in_dim(cot, which, 1, False).reshape(n_col // 2 * tokens, -1)

    partial = lax.dot_general(pick(col % 2), w_here, NDIMS, preferred_element_type=F32)
    partial = partial + lax.dot_general(
        pick(1 - col % 2), w_next, NDIMS, preferred_element_type=F32
    )
    partial = partial.astype(BF16)

    w_both = jnp.concatenate((w_gate, w_up), axis=0)
    partial, w_both = lax.optimization_barrier((partial, w_both))
    w_both = jnp.concatenate((w_both, swap(w_both)), axis=1)

    planes = n_col // 2
    half = planes // 2
    rank = col // 2

    def chunk(index):
        start = (index + planes) % planes * tokens
        return lax.dynamic_slice_in_dim(partial, start, tokens, 0).astype(F32)

    up_sum = chunk(rank + half).astype(BF16)
    down_grad = jnp.zeros((n_col * tokens, 2 * units), BF16)
    down_sum = chunk(rank - half + 1).astype(BF16)
    for step in range(1, half + 1):
        up_in = hop(up_sum, 2)
        if step == 2:
            down_sum, w_both, down_grad = lax.optimization_barrier((down_sum, w_both, down_grad))
        if step < half:
            down_in = hop(down_sum, -2)
            up_sum = (up_in.astype(F32) + chunk(rank + half - step)).astype(BF16)
            if step < half - 1:
                down_sum = (down_in.astype(F32) + chunk(rank - half + 1 + step)).astype(BF16)
    w_gate2, w_up2 = w_both[: w_gate.shape[0]], w_both[w_gate.shape[0] :]
    mine = (up_in.astype(F32) + down_in.astype(F32) + chunk(rank)).astype(BF16)

    rows = jnp.concatenate((inputs, grad_out), axis=1)
    rows = lax.all_gather(rows, "row", axis=0, tiled=True, axis_index_groups=groups)
    input_rows, cot_rows = rows[:, : inputs.shape[1]], rows[:, inputs.shape[1] :]

    gate_by, up_by, hidden = factors(acts_all, units)

    half = n_col // 2

    def put(whole, piece, index):
        start = (index + n_col) % n_col * tokens
        return lax.dynamic_update_slice_in_dim(whole, piece, start, 0)

    down_grad = put(down_grad, mine, col)
    above = below = mine
    for step in range(1, half + 1):
        above = hop(above, 1)
        if step == half:
            above, gate_by, up_by, hidden = lax.optimization_barrier(
                (above, gate_by, up_by, hidden)
            )
        if step < half:
            below = hop(below, -1)
        down_grad = put(down_grad, above, col - step)
        if step < half:
            down_grad = put(down_grad, below, col + step)

    grads = down_grad.astype(F32)
    gate_grad = (grads * gate_by.astype(F32)).astype(BF16)
    up_grad = (grads * up_by.astype(F32)).astype(BF16)
    total = lax.dot_general(gate_grad, w_gate2, NDIMS, preferred_element_type=F32)
    total = total + lax.dot_general(up_grad, w_up2, NDIMS, preferred_element_type=F32)
    total, gate_grad, up_grad = lax.optimization_barrier(
        (total.astype(BF16), gate_grad, up_grad)
    )
    sums = exchange(total).reshape(chips, tokens, -1)
    input_grad = jnp.sum(sums.astype(F32), axis=0).astype(BF16)

    def over_tokens(left, right):
        return lax.dot_general(left, right, TDIMS, preferred_element_type=F32)

    wd_other = swap(over_tokens(hidden[:, units:], cot_rows).astype(BF16))
    wg_give = over_tokens(input_rows, gate_grad[:, units:]).astype(BF16)
    wu_give = over_tokens(input_rows, up_grad[:, units:]).astype(BF16)
    width = wg_give.shape[0]
    other = swap(jnp.concatenate((wg_give, wu_give), axis=0))
    w_down_grad = (over_tokens(hidden[:, :units], cot_rows) + wd_other.astype(F32)).astype(BF16)
    w_gate_grad = over_tokens(input_rows, gate_grad[:, :units]) + other[:width].astype(F32)
    w_up_grad = over_tokens(input_rows, up_grad[:, :units]) + other[width:].astype(F32)
    w_gate_grad, w_up_grad = w_gate_grad.astype(BF16), w_up_grad.astype(BF16)
    return (input_grad, w_gate_grad, w_up_grad, w_down_grad)


def solution(mesh):
    n_row, n_col = mesh.shape["row"], mesh.shape["col"]

    def step(*arrays):
        return local(n_row, n_col, *arrays)

    return jax.shard_map(
        step,
        mesh=mesh,
        in_specs=(
            P("row", "col"),
            P("col", "row"),
            P("col", "row"),
            P("col", "row"),
            P("col", "row"),
            P("row", "col"),
            P("row", "col"),
        ),
        out_specs=(P("row", "col"), P("col", "row"), P("col", "row"), P("row", "col")),
        check_vma=False,
    )
```
